128 devices in a mesh: terms: 8 (over y, core), blocks: 16 (over z, x).
Axes of the slice: x: 4, y: 4, z: 4, core: 2. Of those that a mesh axis runs over, the one named last changes fastest.
Arguments:
- psi: bfloat16 [2, 4096, 4096], P(None, 'blocks'), may hold values from -6 to 6
- shifts: int32 [48], P('terms'), may hold values from 0 to 15, as said below
- left_ops: bfloat16 [48, 16, 256, 256], P('terms'), may hold values from -0.0546875 to 0.0546875
- right_ops: bfloat16 [48, 16, 256, 256], P('terms'), may hold values from -0.375 to 0.375
Outputs:
- sigma: float32 [2, 4096, 4096], P(None, 'terms', 'blocks')
The draws below stay inside these ranges and needn't reach their ends.
Inputs may be any that keep to these rules, and one draw needn't show every extreme that they name: Term t takes block (i, j + shifts[t]) to block (i + shifts[t], j), sectors counted modulo 16.
All inputs are finite; a program needn't handle non-finite values.
Results may differ from the reference program's by a relative error of at most 0.0029.
Values may be sent and summed in bfloat16 or wider, within the bound.
A program may use at most 256 MiB of HBM per device.

```python
import jax
import jax.numpy as jnp
from jax import lax

B = 256
VECS = 2
SECTORS = 16
TERMS = 48
DIM = 4096


def draw_shifts(key, part):
    key = jax.random.fold_in(key, 7)
    key_values, key_low, key_high = jax.random.split(key, 3)
    values = jax.random.randint(key_values, (TERMS,), 0, SECTORS, dtype=jnp.int32)
    low_at = jax.random.randint(key_low, (), 0, TERMS, dtype=jnp.int32)
    step_high = jax.random.randint(key_high, (), 0, TERMS - 1, dtype=jnp.int32)
    high_at = (low_at + 1 + step_high) % TERMS
    values = values.at[low_at].set(0)
    return values.at[high_at].set(SECTORS - 1)


def level_of(rng, shape, cuts, least, high):
    gain = 1.0
    for dim, parts in cuts:
        draws = jax.random.uniform(jax.random.fold_in(jax.random.fold_in(rng, 6), dim), (parts,), jnp.float32, least / len(cuts), high / len(cuts))
        gain = gain * jnp.repeat(jnp.exp(draws), shape[dim] // parts).reshape((-1,) + (1,) * (len(shape) - 1 - dim))
    return gain


def centred(key, dims, deviation, limit, cuts=(), kind=jnp.bfloat16):
    gain = level_of(key, dims, cuts, -0.22, 0.18) if cuts else 1.0
    values = jax.random.normal(key, dims, jnp.float32) * deviation * gain
    return jnp.minimum(jnp.maximum(values, -limit), limit).astype(kind)


def setup_inputs(seed: int = 0) -> dict:
    key_list = jax.random.split(jax.random.key(seed), 5)
    return {
        "psi": centred(key_list[0], (VECS, DIM, DIM), 1.0, 6.0, ((1, 16),)),
        "shifts": draw_shifts(jax.random.fold_in(key_list[4], 71), 0),
        "left_ops": centred(key_list[2], (TERMS, SECTORS, B, B), (B * TERMS) ** -0.5, 0.0546875, ((0, 8),)),
        "right_ops": centred(key_list[3], (TERMS, SECTORS, B, B), B ** -0.5, 0.375, ((0, 8),)),
    }


def apply_terms(vector, shifts, left_ops, right_ops):
    blocked = vector.reshape(DIM, SECTORS, B).astype(jnp.float32)

    def one_term(term, running):
        offset = shifts[term]
        right_part = right_ops[term].astype(jnp.float32)
        product = jnp.einsum('rnb,nbc->rnc', blocked, right_part).astype(jnp.bfloat16)
        shifted = jnp.roll(product, -offset, axis=1).reshape(SECTORS, B, DIM)
        shifted = jnp.roll(shifted, offset, axis=0).astype(jnp.float32)
        left_part = jnp.roll(left_ops[term], offset, axis=0).astype(jnp.float32)
        return running + jnp.einsum('nab,nbc->nac', left_part, shifted).reshape(DIM, DIM)

    return lax.fori_loop(0, TERMS, one_term, jnp.zeros((DIM, DIM), jnp.float32))


def reference(psi, shifts, left_ops, right_ops):
    results = [apply_terms(psi[member], shifts, left_ops, right_ops) for member in range(VECS)]
    return jnp.stack(results, axis=0)
```

```python
import functools

import jax
import jax.numpy as jnp
from jax import lax
from jax.experimental import pallas as pl
from jax.experimental.pallas import tpu as pltpu
from jax.sharding import PartitionSpec as P

MESH = pl.DeviceIdType.MESH
ANY = pl.BlockSpec(memory_space=pl.ANY)
SMEM = pl.BlockSpec(memory_space=pltpu.SMEM)
VMEM = pl.BlockSpec(memory_space=pltpu.VMEM)
B = 256
MIB = 1024 * 1024


def place():
    terms = lax.axis_index("terms")
    blocks = lax.axis_index("blocks")
    return terms // 2, terms % 2, blocks // 4, blocks % 4


def at(y, core, z, x):
    return (lax.rem(y + 4, 4) * 2 + core, lax.rem(z + 4, 4) * 4 + lax.rem(x + 4, 4))


def remote(source, target, send, recv, device):
    return pltpu.make_async_remote_copy(
        src_ref=source,
        dst_ref=target,
        send_sem=send,
        recv_sem=recv,
        device_id=device,
        device_id_type=MESH,
    )


def greet(devices):
    barrier = pltpu.get_barrier_semaphore()
    for device in devices:
        pl.semaphore_signal(barrier, inc=1, device_id=device, device_id_type=MESH)
    pl.semaphore_wait(barrier, len(devices))


SHARED = 4
DIRECT = 6


def gather_kernel(
    shifts, shift_row, psi, left, right,
    rows, lefts, rights, other_row,
    right_in, picked,
    x_send, x_recv, y_send, y_recv, c_send, c_recv, l_sem, r_sem,
):
    y, core, z, x = place()
    x_up, x_down = at(y, core, z, x + 1), at(y, core, z, x - 1)
    y_up, y_down = at(y + 1, core, z, x), at(y - 1, core, z, x)
    partner = at(y, 1 - core, z, x)
    greet([x_up, x_down, y_up, y_down, partner])

    def item(index, owner):
        if index < 2:
            return 2 * owner + index, 0, 256
        if index < SHARED:
            return 6 + index, pl.multiple_of(owner * 64, 64), 64
        return 6 + index, 0, 256

    def held(index, owner, member, part=None):
        sector, start, count = item(index, owner)
        if part is not None:
            count = count // 2
            start = start + part * count
        return rows.at[sector, lax.rem(member + 4, 4), pl.ds(start, count)]

    def own(index):
        sector, start, count = item(index, y)
        column = pl.multiple_of(sector * B, B) if index < 2 else sector * B
        return psi.at[core, pl.ds(start, count), pl.ds(column, B)]

    waiting = []

    def x_copy(index, kind, source, target, device):
        copy = remote(source, target, x_send.at[index, kind], x_recv.at[index, kind], device)
        copy.start()
        waiting.append(copy)
        return copy

    def y_copy(index, which, kind, source, device):
        copy = remote(
            source, source, y_send.at[index, which, kind], y_recv.at[index, which, kind], device
        )
        copy.start()
        waiting.append(copy)
        return copy

    def x_first(index):
        target = held(index, y, x)
        return (
            x_copy(index, 0, own(index), target, x_up),
            x_copy(index, 1, own(index), target, x_down),
        )

    def x_forward_up(index):
        block = held(index, y, x - 1, 0)
        return x_copy(index, 2, block, block, x_up)

    def x_forward_down(index):
        block = held(index, y, x + 1, 1)
        return x_copy(index, 3, block, block, x_down)

    def y_first(index, which, member):
        block = held(index, y, member)
        return (
            y_copy(index, which, 0, block, y_up),
            y_copy(index, which, 1, block, y_down),
        )

    def y_forward_up(index, which, member):
        return y_copy(index, which, 2, held(index, lax.rem(y + 3, 4), member, 0), y_up)

    def y_forward_down(index, which, member):
        return y_copy(index, which, 3, held(index, lax.rem(y + 1, 4), member, 1), y_down)

    first = [x_first(index) for index in range(SHARED)]
    local = []
    load = pltpu.make_async_copy(right, right_in, r_sem)
    load.start()
    swap = remote(shift_row, other_row, c_send.at[0], c_recv.at[0], partner)
    swap.start()
    waiting.append(swap)
    mine = left.at[:, pl.ds(4 * z, 4)]
    swap_left = remote(mine, lefts.at[pl.ds(6, 6)], c_send.at[1], c_recv.at[1], partner)
    swap_left.start()
    waiting.append(swap_left)
    copy = pltpu.make_async_copy(mine, lefts.at[pl.ds(0, 6)], l_sem.at[0])
    copy.start()
    local.append(copy)
    for sector in range(16):
        copy = pltpu.make_async_copy(
            psi.at[core, :, pl.ds(sector * B, B)], rows.at[sector, x], l_sem.at[1 + sector]
        )
        copy.start()
        local.append(copy)

    members = [x - 1, x + 1, x + 2]
    forward = []
    y_list = {}
    for index in range(SHARED):
        up, down = first[index]
        up.wait_recv()
        one = x_forward_up(index)
        y_list[index, 0] = y_first(index, 0, members[0])
        down.wait_recv()
        two = x_forward_down(index)
        y_list[index, 1] = y_first(index, 1, members[1])
        forward.append((one, two))
    direct = [x_first(index) for index in range(SHARED, SHARED + DIRECT)]

    load.wait()
    for term in range(6):
        shift = shifts[term]
        for k in range(4):
            picked[term, k] = right_in[term, (x + 4 * k + shift) & 15]
    swap_right = remote(picked, rights.at[pl.ds(6, 6)], c_send.at[2], c_recv.at[2], partner)
    swap_right.start()
    waiting.append(swap_right)
    copy = pltpu.make_async_copy(picked, rights.at[pl.ds(0, 6)], l_sem.at[17])
    copy.start()
    local.append(copy)

    for index in range(SHARED):
        for copy in forward[index]:
            copy.wait_recv()
        y_list[index, 2] = y_first(index, 2, members[2])

    last = []

    def y_second(index, which):
        up, down = y_list[index, which]
        up.wait_recv()
        last.append(y_forward_up(index, which, members[which]))
        down.wait_recv()
        last.append(y_forward_down(index, which, members[which]))

    def x_second(index):
        up, down = direct[index - SHARED]
        up.wait_recv()
        last.append(x_forward_up(index))
        down.wait_recv()
        last.append(x_forward_down(index))

    order = [(index, which) for which in range(3) for index in range(SHARED)]
    while order or direct:
        for _ in range(2):
            if order:
                y_second(*order.pop(0))
        index = SHARED + DIRECT - len(direct) if direct else None
        if direct:
            up, down = direct.pop(0)
            up.wait_recv()
            last.append(x_forward_up(index))
            down.wait_recv()
            last.append(x_forward_down(index))
    for copy in last:
        copy.wait_recv()
    swap.wait_recv()
    swap_left.wait_recv()
    swap_right.wait_recv()
    for copy in waiting:
        copy.wait_send()
    for copy in local:
        copy.wait()


def gather(shifts, psi, left, right):
    row = jnp.zeros((8, 128), jnp.int32).at[0, :6].set(shifts)
    half = jnp.bfloat16
    return pl.pallas_call(
        gather_kernel,
        out_shape=(
            jax.ShapeDtypeStruct((16, 4, B, B), half),
            jax.ShapeDtypeStruct((12, 4, B, B), half),
            jax.ShapeDtypeStruct((12, 4, B, B), half),
            jax.ShapeDtypeStruct((8, 128), jnp.int32),
        ),
        in_specs=[SMEM, ANY, ANY, ANY, ANY],
        out_specs=(ANY, ANY, ANY, ANY),
        scratch_shapes=[
            pltpu.VMEM((6, 16, B, B), half),
            pltpu.VMEM((6, 4, B, B), half),
            pltpu.SemaphoreType.DMA((SHARED + DIRECT, 4)),
            pltpu.SemaphoreType.DMA((SHARED + DIRECT, 4)),
            pltpu.SemaphoreType.DMA((SHARED, 3, 4)),
            pltpu.SemaphoreType.DMA((SHARED, 3, 4)),
            pltpu.SemaphoreType.DMA((3,)),
            pltpu.SemaphoreType.DMA((3,)),
            pltpu.SemaphoreType.DMA((18,)),
            pltpu.SemaphoreType.DMA,
        ],
        compiler_params=pltpu.CompilerParams(
            collective_id=0, has_side_effects=True, vmem_limit_bytes=40 * MIB
        ),
        name="gather",
    )(shifts, row, psi, left, right)


def product_kernel(shifts, other_row, place_ref, rows, lefts, rights, out, total, moved):
    term = pl.program_id(0)
    z, x = place_ref[0], place_ref[1]

    @pl.when(term == 0)
    def _():
        total[...] = jnp.zeros_like(total)

    shift = jnp.where(term < 6, shifts[jnp.minimum(term, 5)], other_row[0, jnp.maximum(term - 6, 0)])
    for k in range(4):
        sector = (x + 4 * k + shift) & 15
        moved[k] = jnp.dot(
            rows[sector].reshape(4 * B, B), rights[0, k], preferred_element_type=jnp.float32
        ).astype(jnp.bfloat16)
    for i in range(4):
        row = (4 * z + i + shift) & 15
        for k in range(4):
            total[k, row] += jnp.dot(
                lefts[0, i], moved[k, i * B : (i + 1) * B], preferred_element_type=jnp.float32
            )

    @pl.when(term == 11)
    def _():
        out[...] = total[...].astype(jnp.bfloat16)


def products(shifts, other_row, rows, lefts, rights):
    blocks = lax.axis_index("blocks")
    where = jnp.stack([blocks // 4, blocks % 4]).astype(jnp.int32)
    return pl.pallas_call(
        product_kernel,
        grid=(12,),
        out_shape=jax.ShapeDtypeStruct((4, 16, B, B), jnp.bfloat16),
        in_specs=[
            SMEM,
            SMEM,
            SMEM,
            VMEM,
            pl.BlockSpec((1, 4, B, B), lambda t: (t, 0, 0, 0)),
            pl.BlockSpec((1, 4, B, B), lambda t: (t, 0, 0, 0)),
        ],
        out_specs=VMEM,
        scratch_shapes=[
            pltpu.VMEM((4, 16, B, B), jnp.float32),
            pltpu.VMEM((4, 4 * B, B), jnp.bfloat16),
        ],
        compiler_params=pltpu.CompilerParams(vmem_limit_bytes=56 * MIB),
        name="products",
    )(shifts, other_row, where, rows, lefts, rights)


OFFSETS = (2, 1, -1, 0)


def reduce_kernel(
    part, out, held, relayed, onward, first, second_out, second, sums,
    load, rel_send, rel_recv, fwd_send, fwd_recv, dir_send, dir_recv, two_send, two_recv,
    c_send, c_recv,
):
    y, core, z, x = place()
    partner = at(y, 1 - core, z, x)
    here = ((y, z), (z, y))

    def on_first(half, step):
        return at(y + step, core, z, x) if half == 0 else at(y, core, z + step, x)

    def on_second(half, step):
        return at(y, core, z + step, x) if half == 0 else at(y + step, core, z, x)

    greet([at(y + d, core, z, x) for d in (1, 2, 3)] + [at(y, core, z + d, x) for d in (1, 2, 3)] + [partner])

    def block(ref, half, step, turn, part_of=None):
        a = lax.rem(here[half][0] + step + 4, 4)
        o = lax.rem(here[half][1] + OFFSETS[turn] + 4, 4)
        y_of, z_of = (a, o) if half == 0 else (o, a)
        if part_of is None:
            return ref.at[z_of, y_of, half]
        return ref.at[z_of, y_of, half, pl.ds(part_of * 256, 256)]

    sent = []

    def start(copy):
        copy.start()
        sent.append(copy)
        return copy

    relays, straight = {}, {}
    for turn in range(4):
        for half in range(2):
            up, down = on_first(half, 1), on_first(half, -1)
            relays[half, turn] = tuple(
                start(remote(
                    block(part, half, 2, turn, way), relayed.at[half, way, turn],
                    rel_send.at[half, way, turn], rel_recv.at[half, way, turn], device,
                ))
                for way, device in enumerate((up, down))
            )
            straight[half, turn] = tuple(
                start(remote(
                    block(part, half, step, turn, 1 - way),
                    first.at[half, way, turn, pl.ds((1 - way) * 256, 256)],
                    dir_send.at[half, way, turn], dir_recv.at[half, way, turn], device,
                ))
                for way, step, device in ((0, 1, up), (1, -1, down))
            )
    fill = pltpu.make_async_copy(part, held, load)
    fill.start()
    fill.wait()

    forwards = {}
    for turn in range(4):
        for half in range(2):
            copies = []
            for way, step in ((0, 1), (1, -1)):
                relays[half, turn][way].wait_recv()
                mine = block(held, half, step, turn, way)[...]
                total = mine.astype(jnp.float32) + relayed[half, way, turn].astype(jnp.float32)
                onward[half, way, turn] = total.astype(jnp.bfloat16)
                copies.append(start(remote(
                    onward.at[half, way, turn], first.at[half, way, turn, pl.ds(way * 256, 256)],
                    fwd_send.at[half, way, turn], fwd_recv.at[half, way, turn], on_first(half, step),
                )))
            forwards[half, turn] = copies

    seconds = {}
    for turn in range(4):
        for half in range(2):
            for way in range(2):
                straight[half, turn][way].wait_recv()
                forwards[half, turn][way].wait_recv()
            total = (
                block(held, half, 0, turn)[...].astype(jnp.float32)
                + first[half, 0, turn].astype(jnp.float32)
                + first[half, 1, turn].astype(jnp.float32)
            )
            if turn < 3:
                second_out[half, turn] = total.astype(jnp.bfloat16)
                seconds[half, turn] = start(remote(
                    second_out.at[half, turn], second.at[half, turn],
                    two_send.at[half, turn], two_recv.at[half, turn],
                    on_second(half, OFFSETS[turn]),
                ))
            else:
                sums[half] = total
    for half in range(2):
        for turn in range(3):
            seconds[half, turn].wait_recv()
        sums[half] = (
            sums[half]
            + second[half, 0].astype(jnp.float32)
            + second[half, 1].astype(jnp.float32)
            + second[half, 2].astype(jnp.float32)
        )
    swap = start(remote(sums.at[1 - core], out.at[core], c_send, c_recv, partner))
    out[core] = sums[core]
    swap.wait_recv()
    for copy in sent:
        copy.wait_send()


def reduce(part):
    half = jnp.bfloat16
    dma = pltpu.SemaphoreType.DMA
    return pl.pallas_call(
        reduce_kernel,
        out_shape=jax.ShapeDtypeStruct((2, 512, B), jnp.float32),
        in_specs=[ANY],
        out_specs=VMEM,
        scratch_shapes=[
            pltpu.VMEM((4, 4, 2, 512, B), half),
            pltpu.VMEM((2, 2, 4, B, B), half),
            pltpu.VMEM((2, 2, 4, B, B), half),
            pltpu.VMEM((2, 2, 4, 512, B), half),
            pltpu.VMEM((2, 3, 512, B), half),
            pltpu.VMEM((2, 3, 512, B), half),
            pltpu.VMEM((2, 512, B), jnp.float32),
            dma,
            dma((2, 2, 4)),
            dma((2, 2, 4)),
            dma((2, 2, 4)),
            dma((2, 2, 4)),
            dma((2, 2, 4)),
            dma((2, 2, 4)),
            dma((2, 3)),
            dma((2, 3)),
            dma,
            dma,
        ],
        compiler_params=pltpu.CompilerParams(
            collective_id=1, has_side_effects=True, vmem_limit_bytes=48 * MIB
        ),
        name="reduce",
    )(part.reshape(4, 4, 2, 512, B))


def per_device(psi, shifts, left_ops, right_ops):
    rows, lefts, rights, other_row = gather(shifts, psi, left_ops, right_ops)
    part = products(shifts, other_row, rows, lefts, rights)
    return reduce(part)


def solution(mesh):
    in_specs = (
        P(None, "blocks", None),
        P("terms"),
        P("terms", None, None, None),
        P("terms", None, None, None),
    )
    out_specs = P(None, "terms", "blocks")
    return jax.shard_map(
        per_device, mesh=mesh, in_specs=in_specs, out_specs=out_specs, check_vma=False
    )
```

```python
import jax
import jax.numpy as jnp
from jax import lax
from jax.experimental import pallas as pl
from jax.experimental.pallas import tpu as pltpu
from jax.sharding import PartitionSpec as P

MESH = pl.DeviceIdType.MESH
B = 256
QUARTER = 64
MIB = 1024 * 1024
F32 = jnp.float32
BF16 = jnp.bfloat16

OFFSETS = (2, 1, -1, 0)
WIDTH = (2, 1)
PIECES = (2, 3)


def wrap(value):
    return lax.rem(value + 4, 4)


def kernel(
    shifts, shift_row, psi, left, right, out,
    q_first, q_last, packed, picked, moved, held, stage_even, stage_odd, shift_all, shift_words,
    far, near, relayed, onward, first, second_out, second,
    x_send, x_recv, z_send, z_recv, y_send, y_recv, d_send, d_recv, o_send, o_recv,
    local_sem, stage_sem, shift_sem,
    rel_send, rel_recv, dir_send, dir_recv, fwd_send, fwd_recv, two_send, two_recv,
):
    q, staged = (q_first, q_last), (stage_even, stage_odd)
    terms = lax.axis_index("terms")
    blocks = lax.axis_index("blocks")
    y, core, z, x = terms // 2, terms % 2, blocks // 4, blocks % 4

    def on(dy=0, dz=0, dx=0):
        return (wrap(y + dy) * 2 + core, wrap(z + dz) * 4 + wrap(x + dx))

    partner = (y * 2 + 1 - core, blocks)
    everyone = [on(dy=d) for d in (1, 2, 3)] + [on(dx=d) for d in (1, 2, 3)]
    everyone += [on(dz=1), on(dz=-1), partner]

    tile = pl.ds(pl.multiple_of(128 * (x // 2), 128), 128)

    def fill_right(term):
        copy = pltpu.make_async_copy(right.at[term], staged[term % 2], stage_sem.at[term])
        copy.start()
        return copy

    def fill_left(pair):
        copies = []
        for k in range(2):
            copy = pltpu.make_async_copy(
                left.at[2 * pair + k, :, :, tile],
                staged[pair % 2].at[:, :, pl.ds(128 * k, 128)],
                stage_sem.at[6 + 2 * pair + k],
            )
            copy.start()
            copies.append(copy)
        return copies

    loads = {0: fill_right(0), 1: fill_right(1)}
    row_copy = pltpu.make_async_copy(shift_row, shift_all.at[0], shift_sem.at[0])
    row_copy.start()
    barrier = pltpu.get_barrier_semaphore()
    for device in everyone:
        pl.semaphore_signal(barrier, inc=1, device_id=device, device_id_type=MESH)
    pl.semaphore_wait(barrier, len(everyone))

    def send(source, target, semaphores, index, device):
        copy = pltpu.make_async_remote_copy(
            src_ref=source,
            dst_ref=target,
            send_sem=semaphores[0],
            recv_sem=semaphores[1].at[index],
            device_id=device,
            device_id_type=MESH,
        )
        copy.start()
        return copy

    xs = [(x_send.at[v], x_recv) for v in range(2)]
    zs = [(z_send.at[v], z_recv) for v in range(2)]
    ys = [(y_send.at[v], y_recv) for v in range(2)]
    ds = [(d_send.at[v], d_recv) for v in range(2)]
    os = [(o_send.at[k], o_recv) for k in range(3)]
    base = 2048 * core
    me = 4 * z + x

    groups = (z, wrap(z - 1), wrap(z + 1), wrap(z + 2))
    state = {}

    def lanes(v, owner):
        return pl.ds(pl.multiple_of(base + 128 * WIDTH[v] * owner, 128), 128 * WIDTH[v])

    def all_lanes(v):
        return pl.ds(pl.multiple_of(base, 128), 512 * WIDTH[v])

    def piece_lanes(v, number):
        width = (2048 - 512 * WIDTH[v]) // PIECES[v]
        return pl.ds(pl.multiple_of(base + 512 * WIDTH[v] + width * number, 128), width)

    def rows_of(v, zz, window, half=None):
        if half is None:
            return q[v].at[pl.ds(4 * zz, 4), :, window]
        return q[v].at[pl.ds(4 * zz + 2 * half, 2), :, window]

    def x_part(v, number, window):
        def source(member):
            return psi.at[v, pl.ds(pl.multiple_of(QUARTER * member, QUARTER), QUARTER), window]

        target = q[v].at[me, :, window]
        copies = [
            send(source(wrap(x + d)), target, xs[v], (v, number, d - 1), on(dx=d)) for d in (1, 3, 2)
        ]
        own = pltpu.make_async_copy(source(x), target, local_sem.at[v, number])
        own.start()
        state["x", v, number] = copies, own

    def x_done(v, number):
        copies, own = state["x", v, number]
        for copy in copies:
            copy.wait_recv()
        own.wait()

    def window_of(v, number):
        return lanes(v, y) if number == 0 else piece_lanes(v, number - 1)

    def x_start(v):
        for number in range(PIECES[v] + 1):
            x_part(v, number, window_of(v, number))

    def z_start(v, number):
        x_done(v, number)
        view = rows_of(v, z, window_of(v, number))
        state["z", v, number] = (
            send(view, view, zs[v], (v, number, 0), on(dz=1)),
            send(view, view, zs[v], (v, number, 1), on(dz=-1)),
        )
        if number == 0:
            y_start(v, 0)

    def y_start(v, g):
        view = rows_of(v, groups[g], lanes(v, y))
        state["y", v, g] = (
            send(view, view, ys[v], (v, g, 0), on(dy=1)),
            send(view, view, ys[v], (v, g, 1), on(dy=-1)),
        )

    def z_pass(v, number):
        window = window_of(v, number)
        up, down = state["z", v, number]
        up.wait_recv()
        view = rows_of(v, groups[1], window, 0)
        one = send(view, view, zs[v], (v, number, 2), on(dz=1))
        if number == 0:
            y_start(v, 1)
        down.wait_recv()
        view = rows_of(v, groups[2], window, 1)
        two = send(view, view, zs[v], (v, number, 3), on(dz=-1))
        if number == 0:
            y_start(v, 2)
        state["zz", v, number] = one, two

    def z_done(v, number):
        for copy in state["zz", v, number]:
            copy.wait_recv()
        if number == 0:
            y_start(v, 3)
        else:
            view = q[v].at[:, :, window_of(v, number)]
            state["d", v, number] = send(view, view, ds[v], (v, number - 1), partner)

    def y_pass(v, g):
        up, down = state["y", v, g]
        up.wait_recv()
        view = rows_of(v, groups[g], lanes(v, wrap(y - 1)), 0)
        one = send(view, view, ys[v], (v, g, 2), on(dy=1))
        down.wait_recv()
        view = rows_of(v, groups[g], lanes(v, wrap(y + 1)), 1)
        state["yy", v, g] = one, send(view, view, ys[v], (v, g, 3), on(dy=-1))

    def y_done(v, g):
        for copy in state["yy", v, g]:
            copy.wait_recv()
        view = rows_of(v, groups[g], all_lanes(v))
        state["d", v, -g] = send(view, view, ds[v], (v, 3 + g), partner)

    def gathered(v):
        for number in range(-3, PIECES[v] + 1):
            state["d", v, number].wait_recv()

    side = x % 2
    lower = lax.broadcasted_iota(jnp.int32, (B, 128), 1) < QUARTER

    def operators():
        swap_row = send(shift_row, shift_all.at[1], os[0], 0, partner)
        for term in range(6):
            loads[term].wait()
            for k in range(4):
                picked[term, k] = staged[term % 2][(4 * z + k + shifts[term]) & 15]
            if term < 4:
                loads[term + 2] = fill_right(term + 2)
            else:
                loads[6 + term - 4] = fill_left(term - 4)
            if term % 2 == 1:
                yield
        swap_right = send(picked.at[pl.ds(0, 6)], picked.at[pl.ds(6, 6)], os[1], 1, partner)
        for pair in range(3):
            slot = pair % 2
            for copy in loads[6 + pair]:
                copy.wait()

            def pack(i, carry, slot=slot, pair=pair):
                odd, even = staged[slot][i, :, 128:], staged[slot][i, :, :128]
                turned = jnp.where(side == 0, odd, even)
                rolled = pltpu.roll(turned.astype(F32), QUARTER, 1).astype(BF16)
                packed[pair, i] = jnp.where(lower == (side == 0), jnp.where(side == 0, even, odd), rolled)
                return carry

            for part in range(2):
                lax.fori_loop(8 * part, 8 * part + 8, pack, 0, unroll=2)
                if part == 1 and pair == 0:
                    loads[8] = fill_left(2)
                yield
        swap_left = send(packed.at[pl.ds(0, 3)], packed.at[pl.ds(3, 3)], os[2], 2, partner)
        row_copy.wait()
        swap_row.wait_recv()
        words = pltpu.make_async_copy(shift_all, shift_words, shift_sem.at[1])
        words.start()
        words.wait()
        yield
        swap_right.wait_recv()
        swap_left.wait_recv()

    def column(v, turn):
        member = wrap(x + OFFSETS[turn])
        sector = 4 * z + member

        def right_products(pair, carry):
            for k in range(2):
                term = 2 * pair + k
                shift = shift_words[term // 6, 0, term % 6]
                window = pl.ds(((sector + shift) & 15) * B, B)
                rows = [
                    q[v][(4 * wrap(y + OFFSETS[u]) + 2 * core + h - shift) & 15, :, window]
                    for u in range(4)
                    for h in range(2)
                ]
                product = jnp.dot(
                    jnp.concatenate(rows, axis=0), picked[term, member], preferred_element_type=F32
                ).astype(BF16)
                place = pl.ds(pl.multiple_of(QUARTER * term, QUARTER), QUARTER)
                for e in range(8):
                    moved[e, place, :] = product[QUARTER * e : QUARTER * (e + 1)]
            return carry

        lax.fori_loop(0, 6, right_products, 0, unroll=6)

        def left_products(e, carry):
            u, h = e // 2, e % 2
            offset = jnp.where(u == 0, 2, jnp.where(u == 1, 1, jnp.where(u == 2, 3, 0)))
            row = 4 * wrap(y + offset) + 2 * core + h
            parts = []
            for pair in range(6):
                one = shift_words[pair // 3, 0, 2 * (pair % 3)]
                two = shift_words[pair // 3, 0, 2 * (pair % 3) + 1]
                parts.append(
                    jnp.where(lower, packed[pair, (row - one) & 15], packed[pair, (row - two) & 15])
                )
            held[turn, e] = jnp.dot(
                jnp.concatenate(parts, axis=1), moved[e], preferred_element_type=F32
            )
            return carry

        lax.fori_loop(0, 8, left_products, 0, unroll=8)

    def along(half, step):
        return on(dy=step) if half == 0 else on(dx=step)

    def across(half, step):
        return on(dx=step) if half == 0 else on(dy=step)

    def value(half, ring, turn, part=None):
        column_turn, row_turn = (turn, ring) if half == 0 else (ring, turn)
        if part is None:
            return held[column_turn, 2 * row_turn + half]
        return held[column_turn, 2 * row_turn + half, 128 * part : 128 * (part + 1)]

    rels, dirs = (rel_send, rel_recv), (dir_send, dir_recv)
    fwds, twos = (fwd_send, fwd_recv), (two_send, two_recv)
    relay, straight, passed, seconds = {}, {}, {}, {}

    def emit(v, half, ring, turn):
        if ring == 0:
            far[v, half, turn] = value(half, 0, turn).astype(BF16)
            for way, step in ((0, 1), (1, -1)):
                relay[v, half, turn, way] = send(
                    far.at[v, half, turn, pl.ds(128 * way, 128)], relayed.at[v, half, way, turn],
                    rels, (v, half, way, turn), along(half, step),
                )
        elif ring < 3:
            way, step = ((0, 1), (1, -1))[ring - 1]
            near[v, half, way, turn] = value(half, ring, turn, 1 - way).astype(BF16)
            straight[v, half, turn, way] = send(
                near.at[v, half, way, turn], first.at[v, half, way, turn, pl.ds(128 * (1 - way), 128)],
                dirs, (v, half, way, turn), along(half, step),
            )

    def add(v, half, turn, way):
        relay[v, half, turn, way].wait_recv()
        total = value(half, 1 + way, turn, way) + relayed[v, half, way, turn].astype(F32)
        onward[v, half, way, turn] = total.astype(BF16)
        passed[v, half, turn, way] = send(
            onward.at[v, half, way, turn], first.at[v, half, way, turn, pl.ds(128 * way, 128)],
            fwds, (v, half, way, turn), along(half, (1, -1)[way]),
        )

    def combine(v, half, turn):
        for way in range(2):
            straight[v, half, turn, way].wait_recv()
            passed[v, half, turn, way].wait_recv()
        total = (
            value(half, 3, turn)
            + first[v, half, 0, turn].astype(F32)
            + first[v, half, 1, turn].astype(F32)
        )
        if turn < 3:
            second_out[v, half, turn] = total.astype(BF16)
            seconds[v, half, turn] = send(
                second_out.at[v, half, turn], second.at[v, half, turn],
                twos, (v, half, turn), across(half, OFFSETS[turn]),
            )
        else:
            out[v, half * B : (half + 1) * B] = total

    def finish(v, half):
        for turn in range(3):
            seconds[v, half, turn].wait_recv()
        rows = slice(half * B, (half + 1) * B)
        out[v, rows] = (
            out[v, rows]
            + second[v, half, 0].astype(F32)
            + second[v, half, 1].astype(F32)
            + second[v, half, 2].astype(F32)
        )

    def spread(v, turn):
        for ring in range(4):
            emit(v, 0, ring, turn)
            emit(v, 1, turn, ring)

    def reduce(v):
        column(v, 0)
        spread(v, 0)
        yield
        column(v, 1)
        spread(v, 1)
        yield
        for way in range(2):
            add(v, 0, 0, way)
        for turn in range(4):
            add(v, 1, turn, 0)
        yield
        column(v, 2)
        spread(v, 2)
        yield
        for way in range(2):
            add(v, 0, 1, way)
        for turn in range(4):
            add(v, 1, turn, 1)
        yield
        column(v, 3)
        spread(v, 3)
        yield
        for turn in (2, 3):
            for way in range(2):
                add(v, 0, turn, way)
            yield
        for turn in range(4):
            for half in range(2):
                combine(v, half, turn)
                yield
        finish(v, 0)
        finish(v, 1)

    ops = operators()

    def go(step, count=1):
        for _ in range(count):
            next(step, None)

    x_start(0)
    go(ops)
    z_start(0, 0)
    z_start(0, 1)
    go(ops)
    z_pass(0, 0)
    z_start(0, 2)
    x_start(1)
    go(ops, 2)
    z_done(0, 0)
    y_pass(0, 0)
    y_pass(0, 1)
    y_pass(0, 2)
    go(ops, 2)
    z_pass(0, 1)
    y_pass(0, 3)
    z_pass(0, 2)
    go(ops, 2)
    for number in range(4):
        z_start(1, number)
    for g in range(4):
        y_done(0, g)
    z_done(0, 1)
    z_done(0, 2)
    go(ops, 9)
    gathered(0)
    first_sum = reduce(0)
    go(first_sum)
    z_pass(1, 0)
    go(first_sum)
    z_done(1, 0)
    go(first_sum)
    for number in range(1, 4):
        z_pass(1, number)
    go(first_sum)
    for g in range(4):
        y_pass(1, g)
    go(first_sum)
    for number in range(1, 4):
        z_done(1, number)
    go(first_sum)
    for g in range(4):
        y_done(1, g)
    go(first_sum, 100)
    gathered(1)
    go(reduce(1), 100)

    def left_all(semaphore, ref):
        pltpu.make_async_copy(ref, ref, semaphore).wait()

    for v in range(2):
        fetched = 2048 - 384 * WIDTH[v]
        left_all(x_send.at[v], q[v].at[pl.ds(0, 3), :, pl.ds(0, fetched)])
        left_all(z_send.at[v], q[v].at[pl.ds(0, 12), :, pl.ds(0, fetched)])
        left_all(y_send.at[v], q[v].at[:, :, pl.ds(0, 384 * WIDTH[v])])
        left_all(d_send.at[v], q[v].at[:, :, pl.ds(0, 2048)])
    left_all(o_send.at[0], shift_row)
    left_all(o_send.at[1], picked.at[pl.ds(0, 6)])
    left_all(o_send.at[2], packed.at[pl.ds(0, 3)])
    left_all(rel_send, relayed)
    left_all(dir_send, near)
    left_all(fwd_send, onward)
    left_all(two_send, second_out)


def per_device(psi, shifts, left_ops, right_ops):
    row = jnp.zeros((8, 128), jnp.int32).at[0, :6].set(shifts)
    dma = pltpu.SemaphoreType.DMA
    some = pl.BlockSpec(memory_space=pl.ANY)
    pairs = [
        (2, 4, 3), (2, 4, 4), (2, 4, 4), (2, 7), (3,),
    ]
    return pl.pallas_call(
        kernel,
        out_shape=jax.ShapeDtypeStruct((2, 512, B), F32),
        in_specs=[pl.BlockSpec(memory_space=pltpu.SMEM), some, some, some, some],
        out_specs=pl.BlockSpec(memory_space=pltpu.VMEM),
        scratch_shapes=[
            pltpu.VMEM((16, QUARTER, 16 * B), BF16),
            pltpu.VMEM((16, QUARTER, 16 * B), BF16),
            pltpu.VMEM((6, 16, B, 128), BF16),
            pltpu.VMEM((12, 4, B, B), BF16),
            pltpu.VMEM((8, 12 * QUARTER, B), BF16),
            pltpu.VMEM((4, 8, B, B), F32),
            pltpu.VMEM((16, B, B), BF16),
            pltpu.VMEM((16, B, B), BF16),
            pltpu.VMEM((2, 8, 128), jnp.int32),
            pltpu.SMEM((2, 8, 128), jnp.int32),
            pltpu.VMEM((2, 2, 4, B, B), BF16),
            pltpu.VMEM((2, 2, 2, 4, 128, B), BF16),
            pltpu.VMEM((2, 2, 2, 4, 128, B), BF16),
            pltpu.VMEM((2, 2, 2, 4, 128, B), BF16),
            pltpu.VMEM((2, 2, 2, 4, B, B), BF16),
            pltpu.VMEM((2, 2, 3, B, B), BF16),
            pltpu.VMEM((2, 2, 3, B, B), BF16),
        ]
        + [dma(shape[:1] if sender else shape) for shape in pairs for sender in (True, False)]
        + [dma((2, 4)), dma((12,)), dma((2,))]
        + [dma, dma((2, 2, 2, 4))] * 3
        + [dma, dma((2, 2, 3))],
        compiler_params=pltpu.CompilerParams(
            collective_id=0, has_side_effects=True, vmem_limit_bytes=62 * MIB
        ),
        name="sigma",
    )(shifts, row, psi, left_ops, right_ops)


def solution(mesh):
    in_specs = (
        P(None, "blocks", None),
        P("terms"),
        P("terms", None, None, None),
        P("terms", None, None, None),
    )
    out_specs = P(None, "terms", "blocks")
    return jax.shard_map(
        per_device, mesh=mesh, in_specs=in_specs, out_specs=out_specs, check_vma=False
    )
```

```python
import jax
import jax.numpy as jnp
from jax import lax
from jax.experimental import pallas as pl
from jax.experimental.pallas import tpu as pltpu
from jax.sharding import PartitionSpec as P

MESH = pl.DeviceIdType.MESH
B = 256
QUARTER = 64
MIB = 1024 * 1024
F32 = jnp.float32
BF16 = jnp.bfloat16

OFFSETS = (2, 1, -1, 0)
WIDTH = (2, 1)
PIECES = (2, 3)


def wrap(value):
    return lax.rem(value + 4, 4)


def kernel(
    shifts, shift_row, psi, left, right, out,
    q_first, q_last, packed, picked, moved, held, stage_even, stage_odd, shift_all, shift_words,
    far, near, relayed, onward, first, second_out, second,
    x_send, x_recv, z_send, z_recv, row_recv, y_send, y_recv, d_send, d_recv, o_send, o_recv,
    local_sem, stage_sem, shift_sem,
    rel_send, rel_recv, dir_send, dir_recv, fwd_send, fwd_recv, two_send, two_recv,
):
    q, staged = (q_first, q_last), (stage_even, stage_odd)
    terms = lax.axis_index("terms")
    blocks = lax.axis_index("blocks")
    y, core, z, x = terms // 2, terms % 2, blocks // 4, blocks % 4

    def on(dy=0, dz=0, dx=0):
        return (wrap(y + dy) * 2 + core, wrap(z + dz) * 4 + wrap(x + dx))

    partner = (y * 2 + 1 - core, blocks)
    everyone = [on(dy=d) for d in (1, 2, 3)] + [on(dx=d) for d in (1, 2, 3)]
    everyone += [on(dz=1), on(dz=-1), partner]

    tile = pl.ds(pl.multiple_of(128 * (x // 2), 128), 128)

    def fill_right(term):
        copy = pltpu.make_async_copy(right.at[term], staged[term % 2], stage_sem.at[term])
        copy.start()
        return copy

    def fill_left(pair):
        copies = []
        for k in range(2):
            copy = pltpu.make_async_copy(
                left.at[2 * pair + k, :, :, tile],
                staged[pair % 2].at[:, :, pl.ds(128 * k, 128)],
                stage_sem.at[6 + 2 * pair + k],
            )
            copy.start()
            copies.append(copy)
        return copies

    loads = {0: fill_right(0), 1: fill_right(1)}
    row_copy = pltpu.make_async_copy(shift_row, shift_all.at[0], shift_sem.at[0])
    row_copy.start()
    barrier = pltpu.get_barrier_semaphore()
    for device in everyone:
        pl.semaphore_signal(barrier, inc=1, device_id=device, device_id_type=MESH)
    pl.semaphore_wait(barrier, len(everyone))

    def send(source, target, semaphores, index, device):
        copy = pltpu.make_async_remote_copy(
            src_ref=source,
            dst_ref=target,
            send_sem=semaphores[0],
            recv_sem=semaphores[1].at[index],
            device_id=device,
            device_id_type=MESH,
        )
        copy.start()
        return copy

    xs = [(x_send.at[v], x_recv) for v in range(2)]
    zs = [(z_send.at[v], z_recv) for v in range(2)]
    ys = [(y_send.at[v], y_recv) for v in range(2)]
    ds = [(d_send.at[v], d_recv) for v in range(2)]
    rs = (z_send.at[0], row_recv)
    os = [(o_send.at[k], o_recv) for k in range(3)]
    base = 2048 * core
    me = 4 * z + x

    groups = (z, wrap(z - 1), wrap(z + 1), wrap(z + 2))
    state = {}

    def lanes(v, owner):
        return pl.ds(pl.multiple_of(base + 128 * WIDTH[v] * owner, 128), 128 * WIDTH[v])

    def all_lanes(v):
        return pl.ds(pl.multiple_of(base, 128), 512 * WIDTH[v])

    def piece_lanes(v, number):
        width = (2048 - 512 * WIDTH[v]) // PIECES[v]
        return pl.ds(pl.multiple_of(base + 512 * WIDTH[v] + width * number, 128), width)

    def rows_of(v, zz, window, half=None):
        if half is None:
            return q[v].at[pl.ds(4 * zz, 4), :, window]
        return q[v].at[pl.ds(4 * zz + 2 * half, 2), :, window]

    def x_part(v, number, window):
        def source(member):
            return psi.at[v, pl.ds(pl.multiple_of(QUARTER * member, QUARTER), QUARTER), window]

        target = q[v].at[me, :, window]
        copies = [
            send(source(wrap(x + d)), target, xs[v], (v, number, d - 1), on(dx=d)) for d in (1, 3, 2)
        ]
        own = pltpu.make_async_copy(source(x), target, local_sem.at[v, number])
        own.start()
        state["x", v, number] = copies, own

    def x_done(v, number):
        copies, own = state["x", v, number]
        for copy in copies:
            copy.wait_recv()
        own.wait()

    def window_of(v, number):
        return lanes(v, y) if number == 0 else piece_lanes(v, number - 1)

    def x_start(v):
        for number in range(PIECES[v] + 1):
            x_part(v, number, window_of(v, number))

    def z_start(v, number):
        x_done(v, number)
        view = rows_of(v, z, window_of(v, number))
        state["z", v, number] = (
            send(view, view, zs[v], (v, number, 0), on(dz=1)),
            send(view, view, zs[v], (v, number, 1), on(dz=-1)),
        )
        if number == 0:
            y_start(v, 0)

    STEPS = (0, 1, 3, 2)

    def row_of(zz, d, window):
        return q[0].at[4 * zz + wrap(x + d), :, window]

    def row_send(number, k, source, target):
        for way, step in ((0, 1), (1, -1)):
            state["r", number, way, k] = send(
                source, target, rs, (number, 4 * way + k), on(dz=step)
            )

    def own_start(number):
        window = window_of(0, number)
        source = psi.at[0, pl.ds(pl.multiple_of(QUARTER * x, QUARTER), QUARTER), window]
        row_send(number, 0, source, row_of(z, 0, window))

    def rows_start(number):
        copies, own = state["x", 0, number]
        for copy, k in ((copies[0], 1), (copies[1], 2), (copies[2], 3)):
            copy.wait_recv()
            view = row_of(z, -STEPS[k], window_of(0, number))
            row_send(number, k, view, view)
        own.wait()
        if number == 0:
            y_start(0, 0)

    def row_pass(number, *which):
        for k in which:
            way, step = ((0, 1), (1, -1))[k // 2]
            state["r", number, way, k].wait_recv()
            view = row_of(groups[1 + way], -STEPS[k], window_of(0, number))
            state["rr", number, k] = send(view, view, rs, (number, 8 + k), on(dz=step))

    def rows_done(number):
        for k in range(4):
            state["r", number, 1 - k // 2, k].wait_recv()
        if number == 0:
            y_start(0, 1)
            y_start(0, 2)

    def y_start(v, g):
        view = rows_of(v, groups[g], lanes(v, y))
        state["y", v, g] = (
            send(view, view, ys[v], (v, g, 0), on(dy=1)),
            send(view, view, ys[v], (v, g, 1), on(dy=-1)),
        )

    def z_pass(v, number):
        window = window_of(v, number)
        up, down = state["z", v, number]
        up.wait_recv()
        view = rows_of(v, groups[1], window, 0)
        one = send(view, view, zs[v], (v, number, 2), on(dz=1))
        if number == 0:
            y_start(v, 1)
        down.wait_recv()
        view = rows_of(v, groups[2], window, 1)
        two = send(view, view, zs[v], (v, number, 3), on(dz=-1))
        if number == 0:
            y_start(v, 2)
        state["zz", v, number] = one, two

    def z_done(v, number):
        for copy in state["zz", v, number] if v else [state["rr", number, k] for k in range(4)]:
            copy.wait_recv()
        if number == 0:
            y_start(v, 3)
        else:
            view = q[v].at[:, :, window_of(v, number)]
            state["d", v, number] = send(view, view, ds[v], (v, number - 1), partner)

    def y_pass(v, g):
        up, down = state["y", v, g]
        up.wait_recv()
        view = rows_of(v, groups[g], lanes(v, wrap(y - 1)), 0)
        one = send(view, view, ys[v], (v, g, 2), on(dy=1))
        down.wait_recv()
        view = rows_of(v, groups[g], lanes(v, wrap(y + 1)), 1)
        state["yy", v, g] = one, send(view, view, ys[v], (v, g, 3), on(dy=-1))

    def y_done(v, g):
        for copy in state["yy", v, g]:
            copy.wait_recv()
        view = rows_of(v, groups[g], all_lanes(v))
        state["d", v, -g] = send(view, view, ds[v], (v, 4 + g), partner)

    def gathered(v):
        for number in range(-3, PIECES[v] + 1):
            state["d", v, number].wait_recv()

    side = x % 2
    lower = lax.broadcasted_iota(jnp.int32, (B, 128), 1) < QUARTER

    def operators():
        swap_row = send(shift_row, shift_all.at[1], os[0], 0, partner)
        for term in range(6):
            loads[term].wait()
            for k in range(4):
                picked[term, k] = staged[term % 2][(4 * z + k + shifts[term]) & 15]
            if term < 4:
                loads[term + 2] = fill_right(term + 2)
            else:
                loads[6 + term - 4] = fill_left(term - 4)
            if term % 2 == 1:
                yield
        swap_right = send(picked.at[pl.ds(0, 6)], picked.at[pl.ds(6, 6)], os[1], 1, partner)
        for pair in range(3):
            slot = pair % 2
            for copy in loads[6 + pair]:
                copy.wait()

            def pack(i, carry, slot=slot, pair=pair):
                odd, even = staged[slot][i, :, 128:], staged[slot][i, :, :128]
                turned = jnp.where(side == 0, odd, even)
                rolled = pltpu.roll(turned.astype(F32), QUARTER, 1).astype(BF16)
                packed[pair, i] = jnp.where(lower == (side == 0), jnp.where(side == 0, even, odd), rolled)
                return carry

            for part in range(2):
                lax.fori_loop(8 * part, 8 * part + 8, pack, 0, unroll=2)
                if part == 1 and pair == 0:
                    loads[8] = fill_left(2)
                yield
        swap_left = send(packed.at[pl.ds(0, 3)], packed.at[pl.ds(3, 3)], os[2], 2, partner)
        row_copy.wait()
        swap_row.wait_recv()
        words = pltpu.make_async_copy(shift_all, shift_words, shift_sem.at[1])
        words.start()
        words.wait()
        yield
        swap_right.wait_recv()
        swap_left.wait_recv()

    def column(v, turn):
        member = wrap(x + OFFSETS[turn])
        sector = 4 * z + member

        def right_products(pair, carry):
            for k in range(2):
                term = 2 * pair + k
                shift = shift_words[term // 6, 0, term % 6]
                window = pl.ds(((sector + shift) & 15) * B, B)
                rows = [
                    q[v][(4 * wrap(y + OFFSETS[u]) + 2 * core + h - shift) & 15, :, window]
                    for u in range(4)
                    for h in range(2)
                ]
                product = jnp.dot(
                    jnp.concatenate(rows, axis=0), picked[term, member], preferred_element_type=F32
                ).astype(BF16)
                place = pl.ds(pl.multiple_of(QUARTER * term, QUARTER), QUARTER)
                for e in range(8):
                    moved[e, place, :] = product[QUARTER * e : QUARTER * (e + 1)]
            return carry

        lax.fori_loop(0, 6, right_products, 0, unroll=6)

        def left_products(e, carry):
            u, h = e // 2, e % 2
            offset = jnp.where(u == 0, 2, jnp.where(u == 1, 1, jnp.where(u == 2, 3, 0)))
            row = 4 * wrap(y + offset) + 2 * core + h
            parts = []
            for pair in range(6):
                one = shift_words[pair // 3, 0, 2 * (pair % 3)]
                two = shift_words[pair // 3, 0, 2 * (pair % 3) + 1]
                parts.append(
                    jnp.where(lower, packed[pair, (row - one) & 15], packed[pair, (row - two) & 15])
                )
            held[turn, e] = jnp.dot(
                jnp.concatenate(parts, axis=1), moved[e], preferred_element_type=F32
            )
            return carry

        lax.fori_loop(0, 8, left_products, 0, unroll=8)

    def along(half, step):
        return on(dy=step) if half == 0 else on(dx=step)

    def across(half, step):
        return on(dx=step) if half == 0 else on(dy=step)

    def value(half, ring, turn, part=None):
        column_turn, row_turn = (turn, ring) if half == 0 else (ring, turn)
        if part is None:
            return held[column_turn, 2 * row_turn + half]
        return held[column_turn, 2 * row_turn + half, 128 * part : 128 * (part + 1)]

    rels, dirs = (rel_send, rel_recv), (dir_send, dir_recv)
    fwds, twos = (fwd_send, fwd_recv), (two_send, two_recv)
    relay, straight, passed, seconds = {}, {}, {}, {}

    def emit(v, half, ring, turn):
        if ring == 0:
            far[v, half, turn] = value(half, 0, turn).astype(BF16)
            for way, step in ((0, 1), (1, -1)):
                relay[v, half, turn, way] = send(
                    far.at[v, half, turn, pl.ds(128 * way, 128)], relayed.at[v, half, way, turn],
                    rels, (v, half, way, turn), along(half, step),
                )
        elif ring < 3:
            way, step = ((0, 1), (1, -1))[ring - 1]
            near[v, half, way, turn] = value(half, ring, turn, 1 - way).astype(BF16)
            straight[v, half, turn, way] = send(
                near.at[v, half, way, turn], first.at[v, half, way, turn, pl.ds(128 * (1 - way), 128)],
                dirs, (v, half, way, turn), along(half, step),
            )

    def add(v, half, turn, way):
        relay[v, half, turn, way].wait_recv()
        total = value(half, 1 + way, turn, way) + relayed[v, half, way, turn].astype(F32)
        onward[v, half, way, turn] = total.astype(BF16)
        passed[v, half, turn, way] = send(
            onward.at[v, half, way, turn], first.at[v, half, way, turn, pl.ds(128 * way, 128)],
            fwds, (v, half, way, turn), along(half, (1, -1)[way]),
        )

    def combine(v, half, turn):
        for way in range(2):
            straight[v, half, turn, way].wait_recv()
            passed[v, half, turn, way].wait_recv()
        total = (
            value(half, 3, turn)
            + first[v, half, 0, turn].astype(F32)
            + first[v, half, 1, turn].astype(F32)
        )
        if turn < 3:
            second_out[v, half, turn] = total.astype(BF16)
            seconds[v, half, turn] = send(
                second_out.at[v, half, turn], second.at[v, half, turn],
                twos, (v, half, turn), across(half, OFFSETS[turn]),
            )
        else:
            out[v, half * B : (half + 1) * B] = total

    def finish(v, half):
        for turn in range(3):
            seconds[v, half, turn].wait_recv()
        rows = slice(half * B, (half + 1) * B)
        out[v, rows] = (
            out[v, rows]
            + second[v, half, 0].astype(F32)
            + second[v, half, 1].astype(F32)
            + second[v, half, 2].astype(F32)
        )

    def spread(v, turn):
        for ring in range(4):
            emit(v, 0, ring, turn)
            emit(v, 1, turn, ring)

    def reduce(v):
        column(v, 0)
        spread(v, 0)
        yield
        column(v, 1)
        spread(v, 1)
        yield
        for way in range(2):
            add(v, 0, 0, way)
        for turn in range(4):
            add(v, 1, turn, 0)
        yield
        column(v, 2)
        spread(v, 2)
        yield
        for way in range(2):
            add(v, 0, 1, way)
        for turn in range(4):
            add(v, 1, turn, 1)
        yield
        column(v, 3)
        spread(v, 3)
        yield
        for turn in (2, 3):
            for way in range(2):
                add(v, 0, turn, way)
            yield
        for turn in range(4):
            for half in range(2):
                combine(v, half, turn)
                yield
        finish(v, 0)
        finish(v, 1)

    ops = operators()

    def go(step, count=1):
        for _ in range(count):
            next(step, None)

    for number in range(3):
        own_start(number)
        x_part(0, number, window_of(0, number))
    go(ops)
    rows_start(0)
    row_pass(0, 0)
    go(ops)
    row_pass(0, 2, 1, 3)
    rows_done(0)
    rows_start(1)
    go(ops)
    z_done(0, 0)
    rows_start(2)
    y_pass(0, 0)
    row_pass(1, 0)
    row_pass(2, 0)
    x_start(1)
    go(ops)
    y_pass(0, 1)
    y_pass(0, 2)
    row_pass(1, 2, 1, 3)
    go(ops)
    y_pass(0, 3)
    row_pass(2, 2, 1, 3)
    z_start(1, 0)
    go(ops)
    for g in range(4):
        y_done(0, g)
    for number in range(1, 4):
        z_start(1, number)
    go(ops)
    rows_done(1)
    z_done(0, 1)
    rows_done(2)
    z_done(0, 2)
    go(ops, 9)
    gathered(0)
    first_sum = reduce(0)
    go(first_sum, 2)
    z_pass(1, 0)
    go(first_sum, 2)
    z_done(1, 0)
    go(first_sum, 2)
    z_pass(1, 1)
    y_pass(1, 0)
    y_pass(1, 1)
    y_pass(1, 2)
    go(first_sum, 2)
    z_pass(1, 2)
    z_pass(1, 3)
    go(first_sum, 2)
    y_pass(1, 3)
    go(first_sum, 2)
    for number in range(1, 4):
        z_done(1, number)
    for g in range(4):
        y_done(1, g)
    gathered(1)
    second_sum = reduce(1)
    go(second_sum, 2)
    go(first_sum, 2)
    go(second_sum, 2)
    go(first_sum, 2)
    go(second_sum, 2)
    go(first_sum, 9)
    go(second_sum, 100)

    def left_all(semaphore, ref):
        pltpu.make_async_copy(ref, ref, semaphore).wait()

    for v in range(2):
        fetched = 2048 - 384 * WIDTH[v]
        left_all(x_send.at[v], q[v].at[pl.ds(0, 3), :, pl.ds(0, fetched)])
        left_all(z_send.at[v], q[v].at[pl.ds(0, 12), :, pl.ds(0, fetched)])
        left_all(y_send.at[v], q[v].at[:, :, pl.ds(0, 384 * WIDTH[v])])
        left_all(d_send.at[v], q[v].at[:, :, pl.ds(0, 2048)])
    left_all(o_send.at[0], shift_row)
    left_all(o_send.at[1], picked.at[pl.ds(0, 6)])
    left_all(o_send.at[2], packed.at[pl.ds(0, 3)])
    left_all(rel_send, relayed)
    left_all(dir_send, near)
    left_all(fwd_send, onward)
    left_all(two_send, second_out)


def per_device(psi, shifts, left_ops, right_ops):
    row = jnp.zeros((8, 128), jnp.int32).at[0, :6].set(shifts)
    dma = pltpu.SemaphoreType.DMA
    some = pl.BlockSpec(memory_space=pl.ANY)
    return pl.pallas_call(
        kernel,
        out_shape=jax.ShapeDtypeStruct((2, 512, B), F32),
        in_specs=[pl.BlockSpec(memory_space=pltpu.SMEM), some, some, some, some],
        out_specs=pl.BlockSpec(memory_space=pltpu.VMEM),
        scratch_shapes=[
            pltpu.VMEM((16, QUARTER, 16 * B), BF16),
            pltpu.VMEM((16, QUARTER, 16 * B), BF16),
            pltpu.VMEM((6, 16, B, 128), BF16),
            pltpu.VMEM((12, 4, B, B), BF16),
            pltpu.VMEM((8, 12 * QUARTER, B), BF16),
            pltpu.VMEM((4, 8, B, B), F32),
            pltpu.VMEM((16, B, B), BF16),
            pltpu.VMEM((16, B, B), BF16),
            pltpu.VMEM((2, 8, 128), jnp.int32),
            pltpu.SMEM((2, 8, 128), jnp.int32),
            pltpu.VMEM((2, 2, 4, B, B), BF16),
            pltpu.VMEM((2, 2, 2, 4, 128, B), BF16),
            pltpu.VMEM((2, 2, 2, 4, 128, B), BF16),
            pltpu.VMEM((2, 2, 2, 4, 128, B), BF16),
            pltpu.VMEM((2, 2, 2, 4, B, B), BF16),
            pltpu.VMEM((2, 2, 3, B, B), BF16),
            pltpu.VMEM((2, 2, 3, B, B), BF16),
        ]
        + [dma((2,)), dma((2, 5, 3)), dma((2,)), dma((2, 4, 4)), dma((4, 12)), dma((2,)), dma((2, 4, 4))]
        + [dma((2,)), dma((2, 8)), dma((3,)), dma((3,))]
        + [dma((2, 5)), dma((12,)), dma((2,))]
        + [dma, dma((2, 2, 2, 4))] * 3
        + [dma, dma((2, 2, 3))],
        compiler_params=pltpu.CompilerParams(
            collective_id=0, has_side_effects=True, vmem_limit_bytes=62 * MIB
        ),
        name="sigma",
    )(shifts, row, psi, left_ops, right_ops)


def solution(mesh):
    in_specs = (
        P(None, "blocks", None),
        P("terms"),
        P("terms", None, None, None),
        P("terms", None, None, None),
    )
    out_specs = P(None, "terms", "blocks")
    return jax.shard_map(
        per_device, mesh=mesh, in_specs=in_specs, out_specs=out_specs, check_vma=False
    )
```

```python
import jax
import jax.numpy as jnp
from jax import lax
from jax.experimental import pallas as pl
from jax.experimental.pallas import tpu as pltpu
from jax.sharding import PartitionSpec as P

MESH = pl.DeviceIdType.MESH
B = 256
QUARTER = 64
MIB = 1024 * 1024
F32 = jnp.float32
BF16 = jnp.bfloat16

OFFSETS = (2, 1, -1, 0)
WIDTH = (2, 1)
PIECES = (2, 3)


def wrap(value):
    return lax.rem(value + 4, 4)


def kernel(
    shifts, shift_row, psi, left, right, out,
    q_first, q_last, packed, picked, moved, held, stage_even, stage_odd, shift_all, shift_words,
    far, near, relayed, onward, first, second_out, second,
    x_send, x_recv, z_send, z_recv, row_recv, y_send, y_recv, d_send, d_recv, o_send, o_recv,
    local_sem, stage_sem, shift_sem,
    rel_send, rel_recv, dir_send, dir_recv, fwd_send, fwd_recv, two_send, two_recv,
):
    q, staged = (q_first, q_last), (stage_even, stage_odd)
    terms = lax.axis_index("terms")
    blocks = lax.axis_index("blocks")
    y, core, z, x = terms // 2, terms % 2, blocks // 4, blocks % 4

    def on(dy=0, dz=0, dx=0):
        return (wrap(y + dy) * 2 + core, wrap(z + dz) * 4 + wrap(x + dx))

    partner = (y * 2 + 1 - core, blocks)
    everyone = [on(dy=d) for d in (1, 2, 3)] + [on(dx=d) for d in (1, 2, 3)]
    everyone += [on(dz=1), on(dz=-1), partner]

    tile = pl.ds(pl.multiple_of(128 * (x // 2), 128), 128)

    def fill_right(term):
        copy = pltpu.make_async_copy(right.at[term], staged[term % 2], stage_sem.at[term])
        copy.start()
        return copy

    def fill_left(pair):
        copies = []
        for k in range(2):
            copy = pltpu.make_async_copy(
                left.at[2 * pair + k, :, :, tile],
                staged[pair % 2].at[:, :, pl.ds(128 * k, 128)],
                stage_sem.at[6 + 2 * pair + k],
            )
            copy.start()
            copies.append(copy)
        return copies

    loads = {0: fill_right(0), 1: fill_right(1)}
    row_copy = pltpu.make_async_copy(shift_row, shift_all.at[0], shift_sem.at[0])
    row_copy.start()
    barrier = pltpu.get_barrier_semaphore()
    for device in everyone:
        pl.semaphore_signal(barrier, inc=1, device_id=device, device_id_type=MESH)
    pl.semaphore_wait(barrier, len(everyone))

    def send(source, target, semaphores, index, device):
        copy = pltpu.make_async_remote_copy(
            src_ref=source,
            dst_ref=target,
            send_sem=semaphores[0],
            recv_sem=semaphores[1].at[index],
            device_id=device,
            device_id_type=MESH,
        )
        copy.start()
        return copy

    xs = [(x_send.at[v], x_recv) for v in range(2)]
    zs = [(z_send.at[v], z_recv) for v in range(2)]
    ys = [(y_send.at[v], y_recv) for v in range(2)]
    ds = [(d_send.at[v], d_recv) for v in range(2)]
    rs = (z_send.at[0], row_recv)
    os = [(o_send.at[k], o_recv) for k in range(5)]
    base = 2048 * core
    me = 4 * z + x

    groups = (z, wrap(z - 1), wrap(z + 1), wrap(z + 2))
    state = {}

    def lanes(v, owner):
        return pl.ds(pl.multiple_of(base + 128 * WIDTH[v] * owner, 128), 128 * WIDTH[v])

    def all_lanes(v):
        return pl.ds(pl.multiple_of(base, 128), 512 * WIDTH[v])

    def piece_lanes(v, number):
        width = (2048 - 512 * WIDTH[v]) // PIECES[v]
        return pl.ds(pl.multiple_of(base + 512 * WIDTH[v] + width * number, 128), width)

    def rows_of(v, zz, window, half=None):
        if half is None:
            return q[v].at[pl.ds(4 * zz, 4), :, window]
        return q[v].at[pl.ds(4 * zz + 2 * half, 2), :, window]

    def x_part(v, number, window):
        def source(member):
            return psi.at[v, pl.ds(pl.multiple_of(QUARTER * member, QUARTER), QUARTER), window]

        target = q[v].at[me, :, window]
        copies = [
            send(source(wrap(x + d)), target, xs[v], (v, number, d - 1), on(dx=d)) for d in (1, 3, 2)
        ]
        own = pltpu.make_async_copy(source(x), target, local_sem.at[v, number])
        own.start()
        state["x", v, number] = copies, own

    def x_done(v, number):
        copies, own = state["x", v, number]
        for copy in copies:
            copy.wait_recv()
        own.wait()

    def window_of(v, number):
        return lanes(v, y) if number == 0 else piece_lanes(v, number - 1)

    def x_start(v):
        for number in range(PIECES[v] + 1):
            x_part(v, number, window_of(v, number))

    def z_start(v, number):
        x_done(v, number)
        view = rows_of(v, z, window_of(v, number))
        state["z", v, number] = (
            send(view, view, zs[v], (v, number, 0), on(dz=1)),
            send(view, view, zs[v], (v, number, 1), on(dz=-1)),
        )
        if number == 0:
            y_start(v, 0)

    STEPS = (0, 1, 3, 2)

    def row_of(zz, d, window):
        return q[0].at[4 * zz + wrap(x + d), :, window]

    def row_send(number, k, source, target):
        for way, step in ((0, 1), (1, -1)):
            state["r", number, way, k] = send(
                source, target, rs, (number, 4 * way + k), on(dz=step)
            )

    def own_start(number):
        window = window_of(0, number)
        source = psi.at[0, pl.ds(pl.multiple_of(QUARTER * x, QUARTER), QUARTER), window]
        row_send(number, 0, source, row_of(z, 0, window))

    def rows_start(number):
        copies, own = state["x", 0, number]
        for copy, k in ((copies[0], 1), (copies[1], 2), (copies[2], 3)):
            copy.wait_recv()
            view = row_of(z, -STEPS[k], window_of(0, number))
            row_send(number, k, view, view)
        own.wait()
        if number == 0:
            y_start(0, 0)

    def row_pass(number, *which):
        for k in which:
            way, step = ((0, 1), (1, -1))[k // 2]
            state["r", number, way, k].wait_recv()
            view = row_of(groups[1 + way], -STEPS[k], window_of(0, number))
            state["rr", number, k] = send(view, view, rs, (number, 8 + k), on(dz=step))

    def rows_done(number):
        for k in range(4):
            state["r", number, 1 - k // 2, k].wait_recv()
        if number == 0:
            y_start(0, 1)
            y_start(0, 2)

    def y_start(v, g):
        view = rows_of(v, groups[g], lanes(v, y))
        state["y", v, g] = (
            send(view, view, ys[v], (v, g, 0), on(dy=1)),
            send(view, view, ys[v], (v, g, 1), on(dy=-1)),
        )

    def z_pass(v, number):
        window = window_of(v, number)
        up, down = state["z", v, number]
        up.wait_recv()
        view = rows_of(v, groups[1], window, 0)
        one = send(view, view, zs[v], (v, number, 2), on(dz=1))
        if number == 0:
            y_start(v, 1)
        down.wait_recv()
        view = rows_of(v, groups[2], window, 1)
        two = send(view, view, zs[v], (v, number, 3), on(dz=-1))
        if number == 0:
            y_start(v, 2)
        state["zz", v, number] = one, two

    def z_done(v, number):
        for copy in state["zz", v, number] if v else [state["rr", number, k] for k in range(4)]:
            copy.wait_recv()
        if number == 0:
            y_start(v, 3)
        else:
            view = q[v].at[:, :, window_of(v, number)]
            state["d", v, number] = send(view, view, ds[v], (v, number - 1), partner)

    def y_pass(v, g):
        up, down = state["y", v, g]
        up.wait_recv()
        view = rows_of(v, groups[g], lanes(v, wrap(y - 1)), 0)
        one = send(view, view, ys[v], (v, g, 2), on(dy=1))
        down.wait_recv()
        view = rows_of(v, groups[g], lanes(v, wrap(y + 1)), 1)
        state["yy", v, g] = one, send(view, view, ys[v], (v, g, 3), on(dy=-1))

    def y_done(v, g):
        for copy in state["yy", v, g]:
            copy.wait_recv()
        view = rows_of(v, groups[g], all_lanes(v))
        state["d", v, -g] = send(view, view, ds[v], (v, 4 + g), partner)

    def gathered(v):
        for number in range(-3, PIECES[v] + 1):
            state["d", v, number].wait_recv()

    side = x % 2
    lower = lax.broadcasted_iota(jnp.int32, (B, 128), 1) < QUARTER

    def operators():
        swap_row = send(shift_row, shift_all.at[1], os[0], 0, partner)
        for term in range(6):
            loads[term].wait()
            for k in range(4):
                picked[term, k] = staged[term % 2][(4 * z + k + shifts[term]) & 15]
            if term < 4:
                loads[term + 2] = fill_right(term + 2)
            else:
                loads[6 + term - 4] = fill_left(term - 4)
            if term % 2 == 1:
                yield
        swap_right = send(picked.at[pl.ds(0, 6)], picked.at[pl.ds(6, 6)], os[1], 1, partner)
        swap_left = []
        for pair in range(3):
            slot = pair % 2
            for copy in loads[6 + pair]:
                copy.wait()

            def pack(i, carry, slot=slot, pair=pair):
                odd, even = staged[slot][i, :, 128:], staged[slot][i, :, :128]
                turned = jnp.where(side == 0, odd, even)
                rolled = pltpu.roll(turned.astype(F32), QUARTER, 1).astype(BF16)
                packed[pair, i] = jnp.where(lower == (side == 0), jnp.where(side == 0, even, odd), rolled)
                return carry

            for part in range(2):
                lax.fori_loop(8 * part, 8 * part + 8, pack, 0, unroll=2)
                if part == 1 and pair == 0:
                    loads[8] = fill_left(2)
                if part == 1:
                    swap_left.append(
                        send(packed.at[pair], packed.at[3 + pair], os[2 + pair], 2 + pair, partner)
                    )
                yield
        row_copy.wait()
        swap_row.wait_recv()
        words = pltpu.make_async_copy(shift_all, shift_words, shift_sem.at[1])
        words.start()
        words.wait()
        yield
        swap_right.wait_recv()
        for swap in swap_left:
            swap.wait_recv()

    def column(v, turn):
        member = wrap(x + OFFSETS[turn])
        sector = 4 * z + member

        def right_products(pair, carry):
            for k in range(2):
                term = 2 * pair + k
                shift = shift_words[term // 6, 0, term % 6]
                window = pl.ds(((sector + shift) & 15) * B, B)
                rows = [
                    q[v][(4 * wrap(y + OFFSETS[u]) + 2 * core + h - shift) & 15, :, window]
                    for u in range(4)
                    for h in range(2)
                ]
                product = jnp.dot(
                    jnp.concatenate(rows, axis=0), picked[term, member], preferred_element_type=F32
                ).astype(BF16)
                place = pl.ds(pl.multiple_of(QUARTER * term, QUARTER), QUARTER)
                for e in range(8):
                    moved[e, place, :] = product[QUARTER * e : QUARTER * (e + 1)]
            return carry

        lax.fori_loop(0, 6, right_products, 0, unroll=6)

        def left_products(e, carry):
            u, h = e // 2, e % 2
            offset = jnp.where(u == 0, 2, jnp.where(u == 1, 1, jnp.where(u == 2, 3, 0)))
            row = 4 * wrap(y + offset) + 2 * core + h
            parts = []
            for pair in range(6):
                one = shift_words[pair // 3, 0, 2 * (pair % 3)]
                two = shift_words[pair // 3, 0, 2 * (pair % 3) + 1]
                parts.append(
                    jnp.where(lower, packed[pair, (row - one) & 15], packed[pair, (row - two) & 15])
                )
            held[turn, e] = jnp.dot(
                jnp.concatenate(parts, axis=1), moved[e], preferred_element_type=F32
            )
            return carry

        lax.fori_loop(0, 8, left_products, 0, unroll=8)

    def along(half, step):
        return on(dy=step) if half == 0 else on(dx=step)

    def across(half, step):
        return on(dx=step) if half == 0 else on(dy=step)

    def value(half, ring, turn, part=None):
        column_turn, row_turn = (turn, ring) if half == 0 else (ring, turn)
        if part is None:
            return held[column_turn, 2 * row_turn + half]
        return held[column_turn, 2 * row_turn + half, 128 * part : 128 * (part + 1)]

    rels, dirs = (rel_send, rel_recv), (dir_send, dir_recv)
    fwds, twos = (fwd_send, fwd_recv), (two_send, two_recv)
    relay, straight, passed, seconds = {}, {}, {}, {}

    def emit(v, half, ring, turn):
        if ring == 0:
            far[v, half, turn] = value(half, 0, turn).astype(BF16)
            for way, step in ((0, 1), (1, -1)):
                relay[v, half, turn, way] = send(
                    far.at[v, half, turn, pl.ds(128 * way, 128)], relayed.at[v, half, way, turn],
                    rels, (v, half, way, turn), along(half, step),
                )
        elif ring < 3:
            way, step = ((0, 1), (1, -1))[ring - 1]
            near[v, half, way, turn] = value(half, ring, turn, 1 - way).astype(BF16)
            straight[v, half, turn, way] = send(
                near.at[v, half, way, turn], first.at[v, half, way, turn, pl.ds(128 * (1 - way), 128)],
                dirs, (v, half, way, turn), along(half, step),
            )

    def add(v, half, turn, way):
        relay[v, half, turn, way].wait_recv()
        total = value(half, 1 + way, turn, way) + relayed[v, half, way, turn].astype(F32)
        onward[v, half, way, turn] = total.astype(BF16)
        passed[v, half, turn, way] = send(
            onward.at[v, half, way, turn], first.at[v, half, way, turn, pl.ds(128 * way, 128)],
            fwds, (v, half, way, turn), along(half, (1, -1)[way]),
        )

    def combine(v, half, turn):
        for way in range(2):
            straight[v, half, turn, way].wait_recv()
            passed[v, half, turn, way].wait_recv()
        total = (
            value(half, 3, turn)
            + first[v, half, 0, turn].astype(F32)
            + first[v, half, 1, turn].astype(F32)
        )
        if turn < 3:
            second_out[v, half, turn] = total.astype(BF16)
            seconds[v, half, turn] = send(
                second_out.at[v, half, turn], second.at[v, half, turn],
                twos, (v, half, turn), across(half, OFFSETS[turn]),
            )
        else:
            out[v, half * B : (half + 1) * B] = total

    def finish(v, half):
        for turn in range(3):
            seconds[v, half, turn].wait_recv()
        rows = slice(half * B, (half + 1) * B)
        out[v, rows] = (
            out[v, rows]
            + second[v, half, 0].astype(F32)
            + second[v, half, 1].astype(F32)
            + second[v, half, 2].astype(F32)
        )

    def spread(v, turn):
        for ring in range(4):
            emit(v, 0, ring, turn)
            emit(v, 1, turn, ring)

    def reduce(v):
        column(v, 0)
        spread(v, 0)
        yield
        column(v, 1)
        spread(v, 1)
        yield
        for way in range(2):
            add(v, 0, 0, way)
        for turn in range(4):
            add(v, 1, turn, 0)
        yield
        column(v, 2)
        spread(v, 2)
        yield
        for way in range(2):
            add(v, 0, 1, way)
        for turn in range(4):
            add(v, 1, turn, 1)
        yield
        column(v, 3)
        spread(v, 3)
        yield
        for turn in (2, 3):
            for way in range(2):
                add(v, 0, turn, way)
            yield
        for turn in range(4):
            for half in range(2):
                combine(v, half, turn)
                yield
        finish(v, 0)
        finish(v, 1)

    ops = operators()

    def go(step, count=1):
        for _ in range(count):
            next(step, None)

    for number in range(3):
        own_start(number)
        x_part(0, number, window_of(0, number))
    go(ops)
    rows_start(0)
    row_pass(0, 0)
    go(ops)
    row_pass(0, 2, 1, 3)
    rows_done(0)
    rows_start(1)
    go(ops)
    z_done(0, 0)
    rows_start(2)
    y_pass(0, 0)
    row_pass(1, 0)
    row_pass(2, 0)
    x_start(1)
    go(ops)
    y_pass(0, 1)
    y_pass(0, 2)
    row_pass(1, 2, 1, 3)
    go(ops)
    y_pass(0, 3)
    row_pass(2, 2, 1, 3)
    z_start(1, 0)
    go(ops)
    for g in range(4):
        y_done(0, g)
    for number in range(1, 4):
        z_start(1, number)
    go(ops, 4)
    rows_done(1)
    z_done(0, 1)
    rows_done(2)
    z_done(0, 2)
    go(ops, 9)
    gathered(0)
    first_sum = reduce(0)
    go(first_sum, 2)
    z_pass(1, 0)
    go(first_sum, 2)
    z_done(1, 0)
    go(first_sum, 2)
    z_pass(1, 1)
    y_pass(1, 0)
    y_pass(1, 1)
    y_pass(1, 2)
    go(first_sum, 2)
    z_pass(1, 2)
    z_pass(1, 3)
    go(first_sum, 2)
    y_pass(1, 3)
    go(first_sum, 2)
    for number in range(1, 4):
        z_done(1, number)
    for g in range(4):
        y_done(1, g)
    gathered(1)
    second_sum = reduce(1)
    go(second_sum, 2)
    go(first_sum, 2)
    go(second_sum, 2)
    go(first_sum, 2)
    go(second_sum, 2)
    go(first_sum, 9)
    go(second_sum, 100)

    def left_all(semaphore, ref):
        pltpu.make_async_copy(ref, ref, semaphore).wait()

    for v in range(2):
        fetched = 2048 - 384 * WIDTH[v]
        left_all(x_send.at[v], q[v].at[pl.ds(0, 3), :, pl.ds(0, fetched)])
        left_all(z_send.at[v], q[v].at[pl.ds(0, 12), :, pl.ds(0, fetched)])
        left_all(y_send.at[v], q[v].at[:, :, pl.ds(0, 384 * WIDTH[v])])
        left_all(d_send.at[v], q[v].at[:, :, pl.ds(0, 2048)])
    left_all(o_send.at[0], shift_row)
    left_all(o_send.at[1], picked.at[pl.ds(0, 6)])
    for pair in range(3):
        left_all(o_send.at[2 + pair], packed.at[pair])
    left_all(rel_send, relayed)
    left_all(dir_send, near)
    left_all(fwd_send, onward)
    left_all(two_send, second_out)


def per_device(psi, shifts, left_ops, right_ops):
    row = jnp.zeros((8, 128), jnp.int32).at[0, :6].set(shifts)
    dma = pltpu.SemaphoreType.DMA
    some = pl.BlockSpec(memory_space=pl.ANY)
    return pl.pallas_call(
        kernel,
        out_shape=jax.ShapeDtypeStruct((2, 512, B), F32),
        in_specs=[pl.BlockSpec(memory_space=pltpu.SMEM), some, some, some, some],
        out_specs=pl.BlockSpec(memory_space=pltpu.VMEM),
        scratch_shapes=[
            pltpu.VMEM((16, QUARTER, 16 * B), BF16),
            pltpu.VMEM((16, QUARTER, 16 * B), BF16),
            pltpu.VMEM((6, 16, B, 128), BF16),
            pltpu.VMEM((12, 4, B, B), BF16),
            pltpu.VMEM((8, 12 * QUARTER, B), BF16),
            pltpu.VMEM((4, 8, B, B), F32),
            pltpu.VMEM((16, B, B), BF16),
            pltpu.VMEM((16, B, B), BF16),
            pltpu.VMEM((2, 8, 128), jnp.int32),
            pltpu.SMEM((2, 8, 128), jnp.int32),
            pltpu.VMEM((2, 2, 4, B, B), BF16),
            pltpu.VMEM((2, 2, 2, 4, 128, B), BF16),
            pltpu.VMEM((2, 2, 2, 4, 128, B), BF16),
            pltpu.VMEM((2, 2, 2, 4, 128, B), BF16),
            pltpu.VMEM((2, 2, 2, 4, B, B), BF16),
            pltpu.VMEM((2, 2, 3, B, B), BF16),
            pltpu.VMEM((2, 2, 3, B, B), BF16),
        ]
        + [dma((2,)), dma((2, 5, 3)), dma((2,)), dma((2, 4, 4)), dma((4, 12)), dma((2,)), dma((2, 4, 4))]
        + [dma((2,)), dma((2, 8)), dma((5,)), dma((5,))]
        + [dma((2, 5)), dma((12,)), dma((2,))]
        + [dma, dma((2, 2, 2, 4))] * 3
        + [dma, dma((2, 2, 3))],
        compiler_params=pltpu.CompilerParams(
            collective_id=0, has_side_effects=True, vmem_limit_bytes=62 * MIB
        ),
        name="sigma",
    )(shifts, row, psi, left_ops, right_ops)


def solution(mesh):
    in_specs = (
        P(None, "blocks", None),
        P("terms"),
        P("terms", None, None, None),
        P("terms", None, None, None),
    )
    out_specs = P(None, "terms", "blocks")
    return jax.shard_map(
        per_device, mesh=mesh, in_specs=in_specs, out_specs=out_specs, check_vma=False
    )
```
